512 devices in a mesh: row: 16 (over y_hi, x), col: 16 (over z, core), cores: 2 (over y_lo).
Axes of the slice: x: 4, y: 8 (y_hi: 4, y_lo: 2; y = y_hi * 2 + y_lo), z: 8, core: 2. Of those that a mesh axis runs over, the one named last changes fastest.
Arguments:
- dtn: bfloat16 [16, 16, 1024, 1024], P('row', 'col'), may hold values from -1.4 to 3.7, as said below
- flux_part: float32 [16, 16, 64, 1024], P('row', 'col', 'cores'), may hold values from -6 to 6
- point_order: int32 [16, 16, 1024], P('row', 'col'), may hold values from 0 to 1023, as said below
- west_values: float32 [16, 16, 64, 256], P('row', 'col', 'cores'), may hold values from -6 to 6
- outer_values: float32 [16, 16, 64, 256], P('row', 'col', 'cores'), may hold values from -6 to 6
- interior_map: float32 [16, 16, 256, 1024], P('row', 'col'), may hold values from -0.1875 to 0.1875
- interior_part: float32 [16, 16, 64, 256], P('row', 'col', 'cores'), may hold values from -6 to 6
Outputs:
- parent_dtn: bfloat16 [16, 16, 768, 1536], P('row', 'col', 'cores')
- parent_flux: float32 [16, 16, 64, 768], P('row', 'col', 'cores')
- interior_values: float32 [16, 16, 64, 256], P('row', 'col', 'cores')
The draws below stay inside these ranges and needn't reach their ends.
Inputs may be any that keep to these rules, and one draw needn't show every extreme that they name: `point_order`: for each box a permutation: entry s * 256 + t is the stored position of the t-th point of side s (south, east, north, west), points of a side by increasing coordinate. `dtn`: each map is symmetric; for two siblings the sum of their blocks on the shared side is symmetric positive definite.
All inputs are finite; a program needn't handle non-finite values.
Results may differ from the reference program's by a relative error of at most 0.001.
Values may be sent and summed in bfloat16 or wider, within the bound.
No kernel may reach another device: no remote copies, remote signals or barrier semaphores. Data moves between devices by JAX's collectives and lax.ppermute only.
A program may use at most 64 MiB of HBM per device.

```python
import math
import jax
import jax.numpy as jnp
from jax import lax

B = 256
LOADS = 64
BOX_ROWS = 16
BOX_COLS = 16


def box_orders(key):
    keys = jax.random.split(key, BOX_ROWS * BOX_COLS)
    perms = jax.vmap(lambda single: jax.random.permutation(single, 4 * B))(keys)
    return perms.reshape(BOX_ROWS, BOX_COLS, 4 * B).astype(jnp.int32)


def draw_point_order(key, part):
    return box_orders(key)


def draw_dtn(key, part):
    orders = box_orders(key).reshape(BOX_ROWS * BOX_COLS, 4 * B)
    key = jax.random.fold_in(key, 11)
    full = 4 * B
    spacing = 1.0 / B
    marks = jnp.arange(full, dtype=jnp.int32)
    sides = marks // B
    along = ((marks % B).astype(jnp.float32) + 0.5) * spacing
    xpos = jnp.where(sides == 0, along, jnp.where(sides == 1, 1.0, jnp.where(sides == 2, along, 0.0)))
    ypos = jnp.where(sides == 0, 0.0, jnp.where(sides == 1, along, jnp.where(sides == 2, 1.0, along)))
    dist_sq = (xpos[:, None] - xpos[None, :]) ** 2 + (ypos[:, None] - ypos[None, :]) ** 2
    on_diagonal = marks[:, None] == marks[None, :]
    across_sides = sides[:, None] != sides[None, :]
    upper_half = marks[:, None] < marks[None, :]
    kernel = jnp.where(on_diagonal, 0.0, spacing * spacing / math.pi / jnp.where(on_diagonal, 1.0, dist_sq))

    def one_box(index):
        box_key = jax.random.fold_in(key, index)
        gain_key, screen_key, noise_key = jax.random.split(box_key, 3)
        gains = jnp.exp(jax.random.uniform(gain_key, (full,), jnp.float32, 0.0, 0.34657))
        screen = jnp.exp(jax.random.uniform(screen_key, (full,), jnp.float32, -5.809143, -4.422849))
        gain_pairs = gains[:, None] * gains[None, :]
        kernel_part = (-(kernel * gain_pairs)).astype(jnp.bfloat16)
        kernel_part = lax.optimization_barrier(kernel_part).astype(jnp.float32)
        noise_draw = jax.random.uniform(noise_key, (full, full), jnp.float32, -0.05, 0.05)
        symmetric = jnp.where(upper_half, noise_draw, noise_draw.T)
        off_diagonal = jnp.where(across_sides, kernel_part + symmetric, kernel_part)
        target = -jnp.sum(kernel_part, axis=1) + screen
        first_diag = lax.optimization_barrier(target.astype(jnp.bfloat16)).astype(jnp.float32)
        bumped = lax.optimization_barrier((first_diag * 1.0078125).astype(jnp.bfloat16)).astype(jnp.float32)
        diagonal_vals = jnp.where(first_diag < target, bumped, first_diag)
        natural = jnp.where(on_diagonal, diagonal_vals[:, None], off_diagonal)
        order = orders[index]
        inverse = jnp.zeros((full,), jnp.int32).at[order].set(jnp.arange(full, dtype=jnp.int32))
        stored = jnp.take(jnp.take(natural, inverse, axis=0), inverse, axis=1)
        return stored.astype(jnp.bfloat16)
    boxes = lax.map(one_box, jnp.arange(BOX_ROWS * BOX_COLS, dtype=jnp.int32))
    return boxes.reshape(BOX_ROWS, BOX_COLS, full, full)


def block_scale(rng, dims, cuts, least, high):
    def one(axis_at, shards_of):
        heights = jax.random.uniform(jax.random.fold_in(jax.random.fold_in(rng, 6), axis_at), (shards_of,), jnp.float32, least / len(cuts), high / len(cuts))
        return jnp.repeat(jnp.exp(heights), dims[axis_at] // shards_of).reshape((-1,) + (1,) * (len(dims) - axis_at - 1))

    factor_of = one(*cuts[0])
    for cut in cuts[1:]:
        factor_of = factor_of * one(*cut)
    return factor_of


def normal_values(own_key, dims, width, reach, cuts=(), kind=jnp.bfloat16):
    values = width * jax.random.normal(own_key, dims, jnp.float32)
    if cuts:
        values = values * block_scale(own_key, dims, cuts, -0.22, 0.18)
    return jnp.clip(values, -reach, reach).astype(kind)


def setup_inputs(seed: int = 0) -> dict:
    key_list = jax.random.split(jax.random.key(seed), 8)
    return {
        "dtn": draw_dtn(jax.random.fold_in(key_list[7], 71), 0),
        "flux_part": normal_values(key_list[1], (BOX_ROWS, BOX_COLS, LOADS, 4 * B), 1.0, 6.0, ((0, 16), (1, 16), (2, 2)), jnp.float32),
        "point_order": draw_point_order(jax.random.fold_in(key_list[7], 71), 0),
        "west_values": normal_values(key_list[3], (BOX_ROWS, BOX_COLS, LOADS, B), 1.0, 6.0, ((0, 16), (1, 16), (2, 2)), jnp.float32),
        "outer_values": normal_values(key_list[4], (BOX_ROWS, BOX_COLS, LOADS, B), 1.0, 6.0, ((0, 16), (1, 16), (2, 2)), jnp.float32),
        "interior_map": normal_values(key_list[5], (BOX_ROWS, BOX_COLS, B, 4 * B), (4 * B) ** -0.5, 0.1875, ((0, 16), (1, 16)), jnp.float32),
        "interior_part": normal_values(key_list[6], (BOX_ROWS, BOX_COLS, LOADS, B), 1.0, 6.0, ((0, 16), (1, 16), (2, 2)), jnp.float32),
    }


def arranged_points(parity, side_len):
    sides = jnp.where(parity == 0, jnp.array([0, 1, 3, 2], jnp.int32), jnp.array([1, 2, 3, 0], jnp.int32))
    marks = jnp.arange(4 * side_len, dtype=jnp.int32)
    return sides[marks // side_len] * side_len + marks % side_len

def box_pieces(dtn_box, order_box, parity, side_len):
    pos = jnp.take(order_box, arranged_points(parity, side_len), axis=0)
    arranged = jnp.take(jnp.take(dtn_box, pos, axis=0), pos, axis=1)
    return (pos, arranged)

def reference(dtn, flux_part, point_order, west_values, outer_values, interior_map, interior_part):
    side_len = dtn.shape[-1] // 4
    three = 3 * side_len
    full = 4 * side_len
    loads = flux_part.shape[2]
    high = lax.Precision.HIGHEST
    east_values = jnp.roll(west_values, -1, axis=1)

    def one_pair(index):
        row_low = 2 * (index // BOX_COLS)
        col = index % BOX_COLS
        rows = (row_low, row_low + 1)
        pieces = [box_pieces(dtn[r, col], point_order[r, col], p, side_len) for p, r in enumerate(rows)]
        system = pieces[0][1][three:, three:].astype(jnp.float32) + pieces[1][1][three:, three:].astype(jnp.float32)
        lower = jnp.linalg.cholesky(system)
        coupling = jnp.concatenate([pieces[0][1][three:, :three], pieces[1][1][three:, :three]], axis=1).astype(jnp.float32)
        solved = jax.scipy.linalg.cho_solve((lower, True), coupling).astype(jnp.bfloat16)
        zeros = jnp.zeros((three, three), jnp.float32)
        parents = []
        knowns = []
        fluxes = []
        applied = []
        for p, r in enumerate(rows):
            arranged = pieces[p][1]
            inner = arranged[:three, :three].astype(jnp.float32)
            block = jnp.concatenate([inner, zeros], axis=1) if p == 0 else jnp.concatenate([zeros, inner], axis=1)
            parents.append((block - jnp.dot(arranged[:three, three:].astype(jnp.float32), solved.astype(jnp.float32), preferred_element_type=jnp.float32)).astype(jnp.bfloat16))
            if p == 0:
                known = jnp.concatenate([outer_values[r, col], east_values[r, col], west_values[r, col]], axis=1)
            else:
                known = jnp.concatenate([east_values[r, col], outer_values[r, col], west_values[r, col]], axis=1)
            knowns.append(known)
            fluxes.append(jnp.take(flux_part[r, col], pieces[p][0], axis=1))
            applied.append(jnp.dot(known, arranged[three:, :three].astype(jnp.float32).T, precision=high))
        edge_sum = fluxes[0][:, three:] + fluxes[1][:, three:]
        total = applied[0] + applied[1] + edge_sum
        answer = jax.scipy.linalg.cho_solve((lower, True), jnp.concatenate([edge_sum, total], axis=0).T).T
        zeta = answer[:loads]
        shared = -answer[loads:]
        parent_flux = []
        values = []
        for p, r in enumerate(rows):
            pos, arranged = pieces[p]
            parent_flux.append(fluxes[p][:, :three] - jnp.dot(zeta, arranged[:three, three:].astype(jnp.float32).T, precision=high))
            boundary = jnp.concatenate([knowns[p], shared], axis=1)
            inverse = jnp.zeros((full,), jnp.int32).at[pos].set(jnp.arange(full, dtype=jnp.int32))
            stored = jnp.take(boundary, inverse, axis=1)
            values.append(jnp.dot(stored, interior_map[r, col].T, precision=high) + interior_part[r, col])
        return (jnp.stack(parents), jnp.stack(parent_flux), jnp.stack(values))
    count = BOX_ROWS // 2 * BOX_COLS
    parents, fluxes, values = lax.map(one_pair, jnp.arange(count, dtype=jnp.int32))

    def place(stack):
        shaped = stack.reshape((BOX_ROWS // 2, BOX_COLS, 2) + stack.shape[2:])
        shaped = jnp.moveaxis(shaped, 2, 1)
        return shaped.reshape((BOX_ROWS, BOX_COLS) + stack.shape[2:])
    return (place(parents), place(fluxes), place(values))
```

```python
import functools

import jax
import jax.numpy as jnp
from jax import lax
from jax.experimental import pallas as pl
from jax.experimental.pallas import tpu as pltpu
from jax.sharding import PartitionSpec as P

B = 256
F32 = jnp.float32
BF16 = jnp.bfloat16
LIMIT = 40 * 1024 * 1024


def dot(a, b):
    return lax.dot_general(a, b, (((1,), (0,)), ((), ())), preferred_element_type=F32)


def dot_t(a, b):
    return lax.dot_general(a, b, (((1,), (1,)), ((), ())), preferred_element_type=F32)


def split(x):
    high = x.astype(BF16)
    return high, (x - high.astype(F32)).astype(BF16)


def product(a, b):
    rows = a.shape[0]
    ah, al = split(a)
    bh, bl = split(b)
    both = dot(jnp.concatenate([ah, al], axis=0), bh)
    return both[:rows] + (both[rows:] + dot(ah, bl))


def parity_of():
    return lax.rem(lax.axis_index("row"), 2)


def selection(order_ref, parity):
    full = order_ref.shape[1]
    low = parity == 0
    sides = [order_ref[:, s * B : (s + 1) * B] for s in range(4)]
    pos = jnp.concatenate(
        [
            jnp.where(low, sides[0], sides[1]),
            jnp.where(low, sides[1], sides[2]),
            sides[3],
            jnp.where(low, sides[2], sides[0]),
        ],
        axis=1,
    )
    column = jnp.broadcast_to(pos, (8, full)).T[:, 0:1]
    marks = lax.broadcasted_iota(jnp.int32, (full, full), 1)
    return jnp.where(column == marks, 1.0, 0.0).astype(BF16)


def gather_kernel(order_ref, dtn_ref, flux_ref, west_ref, outer_ref, s_ref, a_ref, fluxed_ref, map_ref, sem):
    copy = pltpu.make_async_copy(dtn_ref, map_ref, sem)
    copy.start()
    three = 3 * B
    loads = flux_ref.shape[0]
    pick = selection(order_ref, parity_of())
    fh, fl = split(flux_ref[...])
    wh, wl = split(west_ref[...])
    oh, ol = split(outer_ref[...])
    s_ref[B : B + loads, :] = wh
    s_ref[B + loads : B + 2 * loads, :] = wl
    s_ref[B + 2 * loads : B + 3 * loads, :] = ol
    copy.wait()
    rows = dot(pick[three:], map_ref[...]).astype(BF16)
    mine = dot_t(rows, pick)
    s_ref[:B, :] = mine[:, three:].astype(BF16)
    a_ref[:B, :] = mine[:, :three].astype(BF16)
    flux = dot_t(jnp.concatenate([fh, fl], axis=0), pick)
    fluxed_ref[...] = flux[:loads] + flux[loads:]
    a_ref[B:, :B] = flux[:loads, three:].astype(BF16)
    a_ref[B:, B : 2 * B] = flux[loads:, three:].astype(BF16)
    a_ref[B:, 2 * B :] = oh


def middle_kernel(
    order_ref, dtn_ref, imap_ref, part_ref, west_ref, outer_ref, own_ref, sib_ref, coup_ref,
    half_ref, rowsj_ref, xh_ref, xl_ref, mh_ref, ml_ref, base_ref,
    map_ref, pick_ref, x_ref, sem,
):
    copy = pltpu.make_async_copy(dtn_ref, map_ref, sem)
    copy.start()
    three = 3 * B
    loads = part_ref.shape[0]
    parity = parity_of()
    pick_ref[...] = selection(order_ref, parity)
    eye = jnp.where(
        lax.broadcasted_iota(jnp.int32, (B, B), 0) == lax.broadcasted_iota(jnp.int32, (B, B), 1), 1.0, 0.0
    ).astype(F32)

    system = own_ref[:B, :].astype(F32) + sib_ref[:B, :].astype(F32)
    top = jnp.max(jnp.sum(jnp.abs(system), axis=0, keepdims=True), axis=1, keepdims=True)
    alpha = 1.0 / top
    low = 1.0 / 128
    scales = []
    for _ in range(5):
        scales.append(2.0 / (1.0 + low))
        low = 4.0 * low / (1.0 + low) ** 2
    t = system * (alpha * scales[0])
    m = 2.0 * eye - t
    x = m * (alpha * scales[0])
    t = product(t, m)
    for c in scales[1:]:
        m = 2.0 * eye - c * t
        both = product(jnp.concatenate([c * t, c * x], axis=0), m)
        t, x = both[:B], both[B:]
    x = product(x, 2.0 * eye - t)
    res = eye - product(system, x)
    x_ref[...] = x + product(x, res)
    off = jnp.max(jnp.sum(jnp.abs(res), axis=0))

    copy.wait()
    core = lax.axis_index("cores")
    count = half_ref.shape[0]
    start = pl.multiple_of(core * count, count)
    rows = dot(pick_ref[pl.ds(start, count), :], map_ref[...]).astype(BF16)
    block = dot_t(rows, pick_ref[...])
    rows_j = block[:, three:].astype(BF16)
    rowsj_ref[...] = rows_j

    mh, ml = split(imap_ref[...])
    pe = pick_ref[pl.ds(pl.multiple_of(B - parity * B, B), B), :]
    pj = pick_ref[three:, :]
    picked = dot_t(jnp.concatenate([mh, ml], axis=0), jnp.concatenate([pe, pj], axis=0))
    mh_ref[...] = picked[:B].astype(BF16)
    ml_ref[...] = picked[B:].astype(BF16)
    wh, wl = split(west_ref[...])
    oh, ol = split(outer_ref[...])
    po = pick_ref[pl.ds(pl.multiple_of(parity * B, B), B), :]
    pw = pick_ref[2 * B : three, :]
    lhs = jnp.concatenate(
        [jnp.concatenate([oh, ol], axis=0), jnp.concatenate([wh, wl], axis=0)], axis=1
    )
    stored = dot(lhs, jnp.concatenate([po, pw], axis=0)).astype(BF16)
    inner = dot_t(stored, mh)
    base_ref[...] = part_ref[...] + inner[:loads] + (inner[loads:] + dot_t(stored[:loads], ml))

    @pl.when(jnp.logical_not(off < 0.005))
    def _():
        def residual(x):
            return eye - lax.dot_general(
                system, x, (((1,), (0,)), ((), ())), precision=lax.Precision.HIGHEST, preferred_element_type=F32
            )

        def body(state):
            step, _ = state
            x = x_ref[...]
            r = residual(x)
            x_ref[...] = x + lax.dot_general(
                x, r, (((1,), (0,)), ((), ())), precision=lax.Precision.HIGHEST, preferred_element_type=F32
            )
            return step + 1, jnp.max(jnp.sum(jnp.abs(r), axis=0))

        x_ref[...] = eye * alpha
        lax.while_loop(
            lambda state: jnp.logical_and(state[0] < 64, jnp.logical_not(state[1] < 0.001)),
            body,
            (jnp.int32(0), jnp.float32(1.0)),
        )

    xh, xl = split(x_ref[...])
    xh_ref[...] = xh
    xl_ref[...] = xl
    coup = coup_ref[:B, :]
    solved = (dot(xh, coup) + dot(xl, coup)).astype(BF16)
    half_ref[...] = (block[:, :three] - dot(rows_j, solved)).astype(BF16)


def final_kernel(
    own_ref, sib_ref, sibs_ref, half_ref, rowsj_ref, xh_ref, xl_ref, mh_ref, ml_ref, base_ref,
    flux_ref, west_ref, outer_ref, easts_ref,
    parent_ref, pflux_ref, values_ref,
):
    three = 3 * B
    loads = base_ref.shape[0]
    parity = parity_of()
    low = parity == 0
    xh, xl = xh_ref[...], xl_ref[...]
    own = own_ref[:B, :]
    sib = sib_ref[:B, :]
    solved = (dot(xh, sib) + dot(xl, sib)).astype(BF16)
    other = (-dot(rowsj_ref[...], solved)).astype(BF16)
    parent_ref[:, pl.ds(pl.multiple_of(parity * three, three), three)] = half_ref[...]
    parent_ref[:, pl.ds(pl.multiple_of(three - parity * three, three), three)] = other

    eh, el = split(easts_ref[:loads, :])
    seh, sel = split(easts_ref[loads:, :])
    oh, ol = split(outer_ref[...])
    wh, wl = split(west_ref[...])
    soh, sol = sib_ref[B:, 2 * B :], sibs_ref[B + 2 * loads : B + 3 * loads, :]
    swh, swl = sibs_ref[B : B + loads, :], sibs_ref[B + loads : B + 2 * loads, :]
    e = jnp.concatenate([eh, el], axis=0)
    o = jnp.concatenate([oh, ol], axis=0)
    w = jnp.concatenate([wh, wl], axis=0)
    se = jnp.concatenate([seh, sel], axis=0)
    so = jnp.concatenate([soh, sol], axis=0)
    sw = jnp.concatenate([swh, swl], axis=0)
    known = jnp.concatenate([jnp.where(low, o, e), jnp.where(low, e, o), w], axis=1)
    sknown = jnp.concatenate([jnp.where(low, se, so), jnp.where(low, so, se), sw], axis=1)
    applied = dot_t(known, own) + dot_t(sknown, sib)
    edge = flux_ref[:, three:] + (sib_ref[B:, :B].astype(F32) + sib_ref[B:, B : 2 * B].astype(F32))
    total = edge + (applied[:loads] + applied[loads:])
    yh, yl = split(jnp.concatenate([edge, total], axis=0))
    both = dot(jnp.concatenate([yh, yl], axis=0), xh)
    answer = both[: 2 * loads] + (both[2 * loads :] + dot(yh, xl))
    zh, zl = split(answer[:loads])
    moved = dot(jnp.concatenate([zh, zl], axis=0), own)
    pflux_ref[...] = flux_ref[:, :three] - (moved[:loads] + moved[loads:])
    sh, sl = split(-answer[loads:])
    hi = jnp.concatenate([eh, sh], axis=1)
    lo = jnp.concatenate([el, sl], axis=1)
    inner = dot_t(jnp.concatenate([hi, lo], axis=0), mh_ref[...])
    values_ref[...] = base_ref[...] + inner[:loads] + (inner[loads:] + dot_t(hi, ml_ref[...]))


def per_device(dtn, flux_part, point_order, west_values, outer_values, interior_map, interior_part):
    dtn, flux, order = dtn[0, 0], flux_part[0, 0], point_order[0]
    west, outer, imap, part = west_values[0, 0], outer_values[0, 0], interior_map[0, 0], interior_part[0, 0]
    full = dtn.shape[0]
    three = full - B
    loads = west.shape[0]
    count = three // lax.axis_size("cores")
    rows, cols = lax.axis_size("row"), lax.axis_size("col")
    pairs = [(i, i ^ 1) for i in range(rows)]
    shape = jax.ShapeDtypeStruct
    vm = pl.BlockSpec(memory_space=pltpu.VMEM)
    hbm = pl.BlockSpec(memory_space=pl.ANY)
    params = pltpu.CompilerParams(vmem_limit_bytes=LIMIT)

    s_pack, a_pack, fluxed = pl.pallas_call(
        gather_kernel,
        out_shape=(
            shape((B + 3 * loads, B), BF16),
            shape((B + loads, three), BF16),
            shape((loads, full), F32),
        ),
        in_specs=[vm, hbm, vm, vm, vm],
        out_specs=(vm, vm, vm),
        scratch_shapes=[pltpu.VMEM((full, full), BF16), pltpu.SemaphoreType.DMA],
        compiler_params=params,
        cost_estimate=pl.CostEstimate(flops=10**9, bytes_accessed=4 * 10**6, transcendentals=0),
        name="gather_shared",
    )(order, dtn, flux, west, outer)

    s_sib = lax.ppermute(s_pack, "row", pairs)
    a_sib = lax.ppermute(a_pack, "row", pairs)
    west_sib = s_sib[B : B + loads].astype(F32) + s_sib[B + loads : B + 2 * loads].astype(F32)
    wests = jnp.concatenate([west, west_sib], axis=0)
    easts = lax.ppermute(wests, "col", [((i + 1) % cols, i) for i in range(cols)])

    half, rows_j, xh, xl, mh, ml, base = pl.pallas_call(
        middle_kernel,
        out_shape=(
            shape((count, three), BF16),
            shape((count, B), BF16),
            shape((B, B), BF16),
            shape((B, B), BF16),
            shape((B, 2 * B), BF16),
            shape((B, 2 * B), BF16),
            shape((loads, B), F32),
        ),
        in_specs=[vm, hbm, vm, vm, vm, vm, vm, vm, vm],
        out_specs=(vm,) * 7,
        scratch_shapes=[
            pltpu.VMEM((full, full), BF16),
            pltpu.VMEM((full, full), BF16),
            pltpu.VMEM((B, B), F32),
            pltpu.SemaphoreType.DMA,
        ],
        compiler_params=params,
        cost_estimate=pl.CostEstimate(flops=6 * 10**9, bytes_accessed=6 * 10**6, transcendentals=0),
        name="inverse_and_own_block",
    )(order, dtn, imap, part, west, outer, s_pack, s_sib, a_pack)

    parent, pflux, values = pl.pallas_call(
        final_kernel,
        out_shape=(
            shape((count, 2 * three), BF16),
            shape((loads, three), F32),
            shape((loads, B), F32),
        ),
        in_specs=[vm] * 14,
        out_specs=(vm, vm, vm),
        compiler_params=params,
        cost_estimate=pl.CostEstimate(flops=10**9, bytes_accessed=3 * 10**6, transcendentals=0),
        name="merge",
    )(a_pack, a_sib, s_sib, half, rows_j, xh, xl, mh, ml, base, fluxed, west, outer, easts)
    return (parent[None, None], pflux[None, None], values[None, None])


def solution(mesh):
    box = P("row", "col", None, None)
    part = P("row", "col", "cores", None)
    return jax.shard_map(
        per_device,
        mesh=mesh,
        in_specs=(box, part, P("row", "col", None), part, part, box, part),
        out_specs=(part, part, part),
        check_vma=False,
    )
```

```python
import jax
import jax.numpy as jnp
from jax import lax
from jax.experimental import pallas as pl
from jax.experimental.pallas import tpu as pltpu
from jax.sharding import PartitionSpec as P

B = 256
F32 = jnp.float32
BF16 = jnp.bfloat16
LIMIT = 32 * 1024 * 1024


def dot(a, b):
    return lax.dot_general(a, b, (((1,), (0,)), ((), ())), preferred_element_type=F32)


def dot_t(a, b):
    return lax.dot_general(a, b, (((1,), (1,)), ((), ())), preferred_element_type=F32)


def split(x):
    high = x.astype(BF16)
    return high, (x - high.astype(F32)).astype(BF16)


def product(a, b):
    rows = a.shape[0]
    ah, al = split(a)
    bh, bl = split(b)
    both = dot(jnp.concatenate([ah, al], axis=0), bh)
    return both[:rows] + (both[rows:] + dot(ah, bl))


def in_hbm(array):
    return pltpu.with_memory_space_constraint(array, pltpu.HBM)


def parity_of():
    return lax.rem(lax.axis_index("row"), 2)


def selection(order_ref, parity):
    full = order_ref.shape[1]
    low = parity == 0
    sides = [order_ref[:, s * B : (s + 1) * B] for s in range(4)]
    pos = jnp.concatenate(
        [
            jnp.where(low, sides[0], sides[1]),
            jnp.where(low, sides[1], sides[2]),
            sides[3],
            jnp.where(low, sides[2], sides[0]),
        ],
        axis=1,
    )
    column = jnp.broadcast_to(pos, (8, full)).T[:, 0:1]
    marks = lax.broadcasted_iota(jnp.int32, (full, full), 1)
    return jnp.where(column == marks, 1.0, 0.0).astype(BF16)


def gather_kernel(
    order_hbm, dtn_hbm, flux_hbm, west_hbm, outer_hbm,
    s_ref, a_ref, fluxed_ref, pick_ref, map_ref,
    order_ref, flux_ref, west_ref, outer_ref, sems,
):
    copies = [
        pltpu.make_async_copy(source, target, sems.at[i])
        for i, (source, target) in enumerate(
            [
                (order_hbm, order_ref),
                (dtn_hbm, map_ref),
                (flux_hbm, flux_ref),
                (west_hbm, west_ref),
                (outer_hbm, outer_ref),
            ]
        )
    ]
    for copy in copies:
        copy.start()
    three = 3 * B
    loads = flux_ref.shape[0]
    copies[0].wait()
    pick = selection(order_ref, parity_of())
    pick_ref[...] = pick
    copies[1].wait()
    rows = dot(pick[three:], map_ref[...]).astype(BF16)
    mine = dot_t(rows, pick)
    s_ref[:B, :] = mine[:, three:].astype(BF16)
    a_ref[...] = mine[:, :three].astype(BF16)
    copies[2].wait()
    fh, fl = split(flux_ref[...])
    flux = dot_t(jnp.concatenate([fh, fl], axis=0), pick)
    fluxed_ref[...] = flux[:loads] + flux[loads:]
    s_ref[B : B + 2 * loads, :] = flux[:, three:].astype(BF16)
    copies[3].wait()
    copies[4].wait()
    wh, wl = split(west_ref[...])
    oh, ol = split(outer_ref[...])
    s_ref[B + 2 * loads : B + 3 * loads, :] = wh
    s_ref[B + 3 * loads : B + 4 * loads, :] = wl
    s_ref[B + 4 * loads : B + 5 * loads, :] = oh
    s_ref[B + 5 * loads : B + 6 * loads, :] = ol


def own_kernel(
    pick_ref, map_ref, imap_hbm, part_ref, own_ref,
    d_ref, rowsj_ref, mh_ref, ml_ref, base_ref,
    imap_ref, sem,
):
    copy = pltpu.make_async_copy(imap_hbm, imap_ref, sem)
    copy.start()
    three = 3 * B
    loads = part_ref.shape[0]
    parity = parity_of()
    core = lax.axis_index("cores")
    count = d_ref.shape[0]
    start = pl.multiple_of(core * count, count)
    rows = dot(pick_ref[pl.ds(start, count), :], map_ref[...]).astype(BF16)
    block = dot_t(rows, pick_ref[...]).astype(BF16)
    d_ref[...] = block[:, :three]
    rowsj_ref[...] = block[:, three:]

    copy.wait()
    mh, ml = split(imap_ref[...])
    pe = pick_ref[pl.ds(pl.multiple_of(B - parity * B, B), B), :]
    pj = pick_ref[three:, :]
    picked = dot_t(jnp.concatenate([mh, ml], axis=0), jnp.concatenate([pe, pj], axis=0))
    mh_ref[...] = picked[:B].astype(BF16)
    ml_ref[...] = picked[B:].astype(BF16)
    po = pick_ref[pl.ds(pl.multiple_of(parity * B, B), B), :]
    pw = pick_ref[2 * B : three, :]
    west = own_ref[B + 2 * loads : B + 4 * loads, :]
    outer = own_ref[B + 4 * loads :, :]
    stored = dot(jnp.concatenate([outer, west], axis=1), jnp.concatenate([po, pw], axis=0)).astype(BF16)
    inner = dot_t(stored, mh)
    base_ref[...] = part_ref[...] + inner[:loads] + (inner[loads:] + dot_t(stored[:loads], ml))


def inverse_kernel(
    own_ref, sib_ref, coup_ref, d_ref, rowsj_ref, flux_ref,
    parent_hbm, xh_ref, xl_ref, pflux_ref, total_ref,
    x_ref, half_ref, sem,
):
    three = 3 * B
    loads = flux_ref.shape[0]
    parity = parity_of()
    eye = jnp.where(
        lax.broadcasted_iota(jnp.int32, (B, B), 0) == lax.broadcasted_iota(jnp.int32, (B, B), 1), 1.0, 0.0
    ).astype(F32)

    system = own_ref[:B, :].astype(F32) + sib_ref[:B, :].astype(F32)
    top = jnp.max(jnp.sum(jnp.abs(system), axis=0, keepdims=True), axis=1, keepdims=True)
    alpha = 1.0 / top
    low = 1.0 / 128
    scales = []
    for _ in range(5):
        scales.append(2.0 / (1.0 + low))
        low = 4.0 * low / (1.0 + low) ** 2
    t = system * (alpha * scales[0])
    m = 2.0 * eye - t
    x = m * (alpha * scales[0])
    t = product(t, m)
    for c in scales[1:]:
        m = 2.0 * eye - c * t
        both = product(jnp.concatenate([c * t, c * x], axis=0), m)
        t, x = both[:B], both[B:]
    x = product(x, 2.0 * eye - t)
    res = eye - product(system, x)
    x_ref[...] = x + product(x, res)
    off = jnp.max(jnp.sum(jnp.abs(res), axis=0))

    coup = coup_ref[...]
    west = own_ref[B + 2 * loads : B + 4 * loads, :]
    outer = own_ref[B + 4 * loads :, :]
    ao = coup_ref[:, pl.ds(pl.multiple_of(parity * B, B), B)]
    aw = coup[:, 2 * B :]
    applied = dot_t(outer, ao) + dot_t(west, aw)
    flux_sib = sib_ref[B : B + 2 * loads, :].astype(F32)
    edge = flux_ref[:, three:] + (flux_sib[:loads] + flux_sib[loads:])
    total_ref[...] = edge + (applied[:loads] + applied[loads:])

    @pl.when(jnp.logical_not(off < 0.005))
    def _():
        def exact(a, b):
            return lax.dot_general(
                a, b, (((1,), (0,)), ((), ())), precision=lax.Precision.HIGHEST, preferred_element_type=F32
            )

        def body(state):
            step, _ = state
            x = x_ref[...]
            r = eye - exact(system, x)
            x_ref[...] = x + exact(x, r)
            return step + 1, jnp.max(jnp.sum(jnp.abs(r), axis=0))

        x_ref[...] = eye * alpha
        lax.while_loop(
            lambda state: jnp.logical_and(state[0] < 64, jnp.logical_not(state[1] < 0.001)),
            body,
            (jnp.int32(0), jnp.float32(1.0)),
        )

    xh, xl = split(x_ref[...])
    xh_ref[...] = xh
    xl_ref[...] = xl
    solved = (dot(xh, coup) + dot(xl, coup)).astype(BF16)
    half_ref[...] = (d_ref[...].astype(F32) - dot(rowsj_ref[...], solved)).astype(BF16)
    copy = pltpu.make_async_copy(
        half_ref, parent_hbm.at[:, pl.ds(pl.multiple_of(parity * three, three), three)], sem
    )
    copy.start()
    eh, el = split(edge)
    both = dot(jnp.concatenate([eh, el], axis=0), xh)
    zh, zl = split(both[:loads] + (both[loads:] + dot(eh, xl)))
    moved = dot(jnp.concatenate([zh, zl], axis=0), coup)
    pflux_ref[...] = flux_ref[:, :three] - (moved[:loads] + moved[loads:])
    copy.wait()


def merge_kernel(
    _, own_ref, sib_ref, sibs_ref, rowsj_ref, xh_ref, xl_ref, mh_ref, ml_ref, base_ref, total_ref, easts_ref,
    parent_hbm, values_ref,
    half_ref, sem,
):
    three = 3 * B
    loads = base_ref.shape[0]
    parity = parity_of()
    low = parity == 0
    xh, xl = xh_ref[...], xl_ref[...]
    sib = sib_ref[...]
    solved = (dot(xh, sib) + dot(xl, sib)).astype(BF16)
    half_ref[...] = (-dot(rowsj_ref[...], solved)).astype(BF16)
    copy = pltpu.make_async_copy(
        half_ref, parent_hbm.at[:, pl.ds(pl.multiple_of(three - parity * three, three), three)], sem
    )
    copy.start()

    eh, el = split(easts_ref[:loads, :])
    seh, sel = split(easts_ref[loads:, :])
    e = jnp.concatenate([eh, el], axis=0)
    se = jnp.concatenate([seh, sel], axis=0)
    sw = sibs_ref[B + 2 * loads : B + 4 * loads, :]
    so = sibs_ref[B + 4 * loads :, :]
    sknown = jnp.concatenate([jnp.where(low, se, so), jnp.where(low, so, se), sw], axis=1)
    ae = own_ref[:, pl.ds(pl.multiple_of(B - parity * B, B), B)]
    applied = dot_t(e, ae) + dot_t(sknown, sib)
    total = total_ref[...] + (applied[:loads] + applied[loads:])
    yh, yl = split(total)
    both = dot(jnp.concatenate([yh, yl], axis=0), xh)
    sh, sl = split(-(both[:loads] + (both[loads:] + dot(yh, xl))))
    hi = jnp.concatenate([eh, sh], axis=1)
    lo = jnp.concatenate([el, sl], axis=1)
    inner = dot_t(jnp.concatenate([hi, lo], axis=0), mh_ref[...])
    values_ref[...] = base_ref[...] + inner[:loads] + (inner[loads:] + dot_t(hi, ml_ref[...]))
    copy.wait()


def per_device(dtn, flux_part, point_order, west_values, outer_values, interior_map, interior_part):
    dtn, flux, order = dtn[0, 0], flux_part[0, 0], point_order[0]
    west, outer, imap, part = west_values[0, 0], outer_values[0, 0], interior_map[0, 0], interior_part[0, 0]
    full = dtn.shape[0]
    three = full - B
    loads = west.shape[0]
    count = three // lax.axis_size("cores")
    rows, cols = lax.axis_size("row"), lax.axis_size("col")
    pairs = [(i, i ^ 1) for i in range(rows)]
    shape = jax.ShapeDtypeStruct
    vm = pl.BlockSpec(memory_space=pltpu.VMEM)
    hbm = pl.BlockSpec(memory_space=pltpu.HBM)
    params = pltpu.CompilerParams(vmem_limit_bytes=LIMIT)
    dma = pltpu.SemaphoreType.DMA

    def cost(flops, moved):
        return pl.CostEstimate(flops=flops, bytes_accessed=moved, transcendentals=0)

    s_pack, a_pack, fluxed, pick, held = pl.pallas_call(
        gather_kernel,
        out_shape=(
            shape((B + 6 * loads, B), BF16),
            shape((B, three), BF16),
            shape((loads, full), F32),
            shape((full, full), BF16),
            shape((full, full), BF16),
        ),
        in_specs=[hbm] * 5,
        out_specs=(vm,) * 5,
        scratch_shapes=[
            pltpu.VMEM(order.shape, jnp.int32),
            pltpu.VMEM(flux.shape, F32),
            pltpu.VMEM(west.shape, F32),
            pltpu.VMEM(outer.shape, F32),
            dma((5,)),
        ],
        compiler_params=params,
        cost_estimate=cost(10**9, 4 * 10**6),
        name="gather_shared",
    )(*[in_hbm(array) for array in (order, dtn, flux, west, outer)])

    s_sib = lax.ppermute(s_pack, "row", pairs)
    a_sib = lax.ppermute(a_pack, "row", pairs)
    at = B + 2 * loads
    west_sib = s_sib[at : at + loads].astype(F32) + s_sib[at + loads : at + 2 * loads].astype(F32)
    wests = jnp.concatenate([west, west_sib], axis=0)
    easts = lax.ppermute(wests, "col", [((i + 1) % cols, i) for i in range(cols)])

    d, rows_j, mh, ml, base = pl.pallas_call(
        own_kernel,
        out_shape=(
            shape((count, three), BF16),
            shape((count, B), BF16),
            shape((B, 2 * B), BF16),
            shape((B, 2 * B), BF16),
            shape((loads, B), F32),
        ),
        in_specs=[vm, vm, hbm, vm, vm],
        out_specs=(vm,) * 5,
        scratch_shapes=[pltpu.VMEM(imap.shape, F32), dma],
        compiler_params=params,
        cost_estimate=cost(3 * 10**9, 10**6),
        name="own_block",
    )(pick, held, in_hbm(imap), part, s_pack)

    parent, xh, xl, pflux, total = pl.pallas_call(
        inverse_kernel,
        out_shape=(
            shape((count, 2 * three), BF16),
            shape((B, B), BF16),
            shape((B, B), BF16),
            shape((loads, three), F32),
            shape((loads, B), F32),
        ),
        in_specs=[vm] * 6,
        out_specs=(hbm, vm, vm, vm, vm),
        scratch_shapes=[pltpu.VMEM((B, B), F32), pltpu.VMEM((count, three), BF16), dma],
        compiler_params=params,
        cost_estimate=cost(4 * 10**9, 10**6),
        name="inverse",
    )(s_pack, s_sib, a_pack, d, rows_j, fluxed)

    parent, values = pl.pallas_call(
        merge_kernel,
        out_shape=(shape((count, 2 * three), BF16), shape((loads, B), F32)),
        in_specs=[hbm] + [vm] * 11,
        out_specs=(hbm, vm),
        scratch_shapes=[pltpu.VMEM((count, three), BF16), dma],
        input_output_aliases={0: 0},
        compiler_params=params,
        cost_estimate=cost(10**9, 10**6),
        name="merge",
    )(parent, a_pack, a_sib, s_sib, rows_j, xh, xl, mh, ml, base, total, easts)
    return (parent[None, None], pflux[None, None], values[None, None])


def solution(mesh):
    box = P("row", "col", None, None)
    part = P("row", "col", "cores", None)
    return jax.shard_map(
        per_device,
        mesh=mesh,
        in_specs=(box, part, P("row", "col", None), part, part, box, part),
        out_specs=(part, part, part),
        check_vma=False,
    )
```

```python
import functools

import jax
import jax.numpy as jnp
from jax import lax
from jax.experimental import pallas as pl
from jax.experimental.pallas import tpu as pltpu
from jax.sharding import PartitionSpec as P

B = 256
F32 = jnp.float32
BF16 = jnp.bfloat16
LIMIT = 32 * 1024 * 1024
SYSTEM = 3 * B // 4


def dot(a, b):
    return lax.dot_general(a, b, (((1,), (0,)), ((), ())), preferred_element_type=F32)


def dot_t(a, b):
    return lax.dot_general(a, b, (((1,), (1,)), ((), ())), preferred_element_type=F32)


def split(x):
    high = x.astype(BF16)
    return high, (x - high.astype(F32)).astype(BF16)


def timed(a, b):
    rows = a.shape[0]
    both = dot(jnp.concatenate(split(a), axis=0), b)
    return both[:rows] + both[rows:]


def in_hbm(array):
    return pltpu.with_memory_space_constraint(array, pltpu.HBM)


def parity_of():
    return lax.rem(lax.axis_index("row"), 2)


def positions(order_ref, parity):
    low = parity == 0
    sides = [order_ref[:, s * B : (s + 1) * B] for s in range(4)]
    pos = jnp.concatenate(
        [
            jnp.where(low, sides[0], sides[1]),
            jnp.where(low, sides[1], sides[2]),
            sides[3],
            jnp.where(low, sides[2], sides[0]),
        ],
        axis=1,
    )
    return jnp.broadcast_to(pos, (8, pos.shape[1])).T[:, 0:1]


def one_hot(column, full):
    marks = lax.broadcasted_iota(jnp.int32, (column.shape[0], full), 1)
    return jnp.where(column == marks, 1.0, 0.0).astype(BF16)


def gather_kernel(
    order_hbm, dtn_hbm, flux_hbm, west_hbm, outer_hbm,
    s_ref, a_ref, fluxed_ref, pick_ref, map_ref,
    order_ref, flux_ref, west_ref, outer_ref, sems,
):
    copies = [
        pltpu.make_async_copy(source, target, sems.at[i])
        for i, (source, target) in enumerate(
            [
                (order_hbm, order_ref),
                (dtn_hbm, map_ref),
                (flux_hbm, flux_ref),
                (west_hbm, west_ref),
                (outer_hbm, outer_ref),
            ]
        )
    ]
    for copy in copies:
        copy.start()
    three = 3 * B
    loads = flux_ref.shape[0]
    copies[0].wait()
    pick = one_hot(positions(order_ref, parity_of()), map_ref.shape[0])
    pick_ref[...] = pick
    copies[1].wait()
    rows = dot(pick[three:], map_ref[...]).astype(BF16)
    copies[2].wait()
    fh, fl = split(flux_ref[...])
    mine = dot_t(jnp.concatenate([rows, fh, fl], axis=0), pick)
    half = B // 2
    block = mine[:B, three:].astype(BF16)
    s_ref[:half, :half] = block[:half, :half]
    s_ref[:half, half:] = block[half:, half:]
    s_ref[half : B - half // 2, :half] = block[half : B - half // 2, :half]
    s_ref[half : B - half // 2, half:] = block[B - half // 2 :, :half]
    a_ref[:B, :] = mine[:B, :three].astype(BF16)
    flux = mine[B:]
    fluxed_ref[...] = flux[:loads] + flux[loads:]
    s_ref[SYSTEM : SYSTEM + 2 * loads, :] = flux[:, three:].astype(BF16)
    copies[3].wait()
    copies[4].wait()
    wh, wl = split(west_ref[...])
    oh, ol = split(outer_ref[...])
    s_ref[SYSTEM + 2 * loads : SYSTEM + 3 * loads, :] = wh
    s_ref[SYSTEM + 3 * loads :, :] = wl
    a_ref[B:, :B] = oh
    a_ref[B:, B : 2 * B] = ol
    a_ref[B:, 2 * B :] = jnp.zeros_like(ol)


def own_body(pick_ref, map_ref, imap_hbm, d_ref, rowsj_ref, mh_ref, ml_ref, ih_ref, il_ref, imap_ref, sem):
    copy = pltpu.make_async_copy(imap_hbm, imap_ref, sem)
    copy.start()
    three = 3 * B
    count = d_ref.shape[0]
    start = pl.multiple_of(lax.axis_index("cores") * count, count)
    rows = dot(pick_ref[pl.ds(start, count), :], map_ref[...]).astype(BF16)
    block = dot_t(rows, pick_ref[...]).astype(BF16)
    d_ref[...] = block[:, :three]
    rowsj_ref[...] = block[:, three:]

    copy.wait()
    mh, ml = split(imap_ref[...])
    ih_ref[...] = mh
    il_ref[...] = ml
    pe = pick_ref[pl.ds(pl.multiple_of(B - parity_of() * B, B), B), :]
    picked = dot_t(jnp.concatenate([mh, ml], axis=0), jnp.concatenate([pe, pick_ref[three:, :]], axis=0))
    mh_ref[...] = picked[:B].astype(BF16)
    ml_ref[...] = picked[B:].astype(BF16)


def system_of(own_ref, sib_ref):
    half = B // 2
    parts = own_ref[:SYSTEM, :].astype(F32) + sib_ref[:SYSTEM, :].astype(F32)
    low = jnp.concatenate([parts[half:, :half], parts[half:, half:]], axis=0)
    return jnp.concatenate(
        [
            jnp.concatenate([parts[:half, :half], low.T], axis=1),
            jnp.concatenate([low, parts[:half, half:]], axis=1),
        ],
        axis=0,
    )


def inverse_body(
    d_ref, rowsj_ref, ih_ref, il_ref, own_ref, sib_ref, coup_ref, flux_ref, pick_ref, part_ref,
    half_ref, xh_ref, xl_ref, pflux_ref, total_ref, base_ref,
    x_ref,
):
    three = 3 * B
    loads = flux_ref.shape[0]
    parity = parity_of()
    coup = coup_ref[:B, :]
    west = own_ref[SYSTEM + 2 * loads :, :]
    outer = jnp.concatenate([coup_ref[B:, :B], coup_ref[B:, B : 2 * B]], axis=0)
    eye = jnp.where(
        lax.broadcasted_iota(jnp.int32, (B, B), 0) == lax.broadcasted_iota(jnp.int32, (B, B), 1), 1.0, 0.0
    ).astype(F32)

    system = system_of(own_ref, sib_ref)
    top = jnp.max(jnp.sum(jnp.abs(system), axis=0, keepdims=True), axis=1, keepdims=True)
    alpha = 1.0 / top
    low = 1.0 / 128
    scales = []
    for _ in range(5):
        scales.append(2.0 / (1.0 + low))
        low = 4.0 * low / (1.0 + low) ** 2

    def first(state):
        t = system * (alpha * scales[0])
        n = (eye - t).astype(BF16)
        return t + timed(t, n), (alpha * scales[0]) * (eye + n.astype(F32))

    def step(c):
        def one(state):
            both = c * jnp.concatenate(state, axis=0)
            n = (eye - both[:B]).astype(BF16)
            both = both + timed(both, n)
            return both[:B], both[B:]

        return one

    po = pick_ref[pl.ds(pl.multiple_of(parity * B, B), B), :]
    pw = pick_ref[2 * B : three, :]
    mh = ih_ref[...]
    state = first(None)
    stored = dot(outer, po)
    state = step(scales[1])(state)
    stored = (stored + dot(west, pw)).astype(BF16)
    state = step(scales[2])(state)
    inner = dot_t(stored, mh)
    state = step(scales[3])(state)
    base_ref[...] = part_ref[...] + inner[:loads] + (inner[loads:] + dot_t(stored[:loads], il_ref[...]))
    t, x = step(scales[4])(state)
    x = x + timed(x, (eye - t).astype(BF16))
    sh, sl = split(system)
    xh, xl = split(x)
    high = dot(jnp.concatenate([sh, sl], axis=0), xh)
    res = eye - (high[:B] + (high[B:] + dot(sh, xl)))

    ao = coup_ref[:B, pl.ds(pl.multiple_of(parity * B, B), B)]
    aw = coup[:, 2 * B :]
    applied = dot_t(outer, ao) + dot_t(west, aw)
    x_ref[...] = x + dot(xh, res.astype(BF16))
    off = jnp.max(jnp.sum(jnp.abs(res), axis=0))
    flux_sib = sib_ref[SYSTEM : SYSTEM + 2 * loads, :].astype(F32)
    edge = flux_ref[:, three:] + (flux_sib[:loads] + flux_sib[loads:])
    total_ref[...] = edge + (applied[:loads] + applied[loads:])

    @pl.when(jnp.logical_not(off < 0.005))
    def _():
        def exact(a, b):
            return lax.dot_general(
                a, b, (((1,), (0,)), ((), ())), precision=lax.Precision.HIGHEST, preferred_element_type=F32
            )

        def body(state):
            step, _ = state
            x = x_ref[...]
            r = eye - exact(system, x)
            x_ref[...] = x + exact(x, r)
            return step + 1, jnp.max(jnp.sum(jnp.abs(r), axis=0))

        x_ref[...] = eye * alpha
        lax.while_loop(
            lambda state: jnp.logical_and(state[0] < 64, jnp.logical_not(state[1] < 0.001)),
            body,
            (jnp.int32(0), jnp.float32(1.0)),
        )

    xh, xl = split(x_ref[...])
    xh_ref[...] = xh
    xl_ref[...] = xl
    eh, el = split(edge)
    both = dot(jnp.concatenate([eh, el], axis=0), xh)
    zeta = both[:loads] + (both[loads:] + dot(eh, xl))
    solved = (dot(xh, coup) + dot(xl, coup)).astype(BF16)
    zh, zl = split(zeta)
    moved = dot(jnp.concatenate([zh, zl], axis=0), coup)
    half_ref[...] = (d_ref[...].astype(F32) - dot(rowsj_ref[...], solved)).astype(BF16)
    pflux_ref[...] = flux_ref[:, :three] - (moved[:loads] + moved[loads:])


def late_block():
    row, col, core = lax.axis_index("row"), lax.axis_index("col"), lax.axis_index("cores")
    return jnp.logical_or(col == lax.axis_size("col") - 1, row + col + core == 0)


def late_inverse():
    return jnp.logical_or(late_block(), lax.axis_index("col") == lax.axis_size("col") - 2)


def block_kernel(late, *refs):
    there = late_block()

    @pl.when(there if late else jnp.logical_not(there))
    def _():
        own_body(*refs)


def early_inverse_kernel(*refs):
    @pl.when(jnp.logical_not(late_inverse()))
    def _():
        inverse_body(*refs)


def late_inverse_kernel(*refs):
    there = late_block()

    @pl.when(there)
    def _():
        inverse_body(*refs[4:])

    @pl.when(jnp.logical_and(late_inverse(), jnp.logical_not(there)))
    def _():
        inverse_body(*refs[:4], *refs[8:])


def merge_kernel(own_ref, sib_ref, sibs_ref, easts_ref, *refs):
    first, second, (parent_hbm, pflux_ref, values_ref, other_ref, sems) = refs[:9], refs[9:18], refs[18:]
    three = 3 * B
    loads = values_ref.shape[0]
    parity = parity_of()
    low = parity == 0
    here, there = late_inverse(), late_block()
    target = parent_hbm.at[:, pl.ds(pl.multiple_of(parity * three, three), three)]
    copies = [pltpu.make_async_copy(first[0], target, sems.at[3])]

    @pl.when(jnp.logical_not(here))
    def _():
        copies[0].start()

    @pl.when(here)
    def _():
        pltpu.make_async_copy(second[0], target, sems.at[3]).start()

    xh, xl, pflux, total, base = [jnp.where(here, b[...], a[...]) for a, b in zip(first[1:6], second[1:6])]
    rows_j, mh, ml = [jnp.where(there, b[...], a[...]) for a, b in zip(first[6:], second[6:])]
    pflux_ref[...] = pflux
    sib = sib_ref[:B, :]
    at = pl.multiple_of(three - parity * three, B)
    size = other_ref.shape[0] // 3

    def other(i):
        part = slice(i * size, (i + 1) * size)
        other_ref[part] = (-dot(rows_j[part], solved)).astype(BF16)
        copies.append(pltpu.make_async_copy(other_ref.at[part], parent_hbm.at[part, pl.ds(at, three)], sems.at[i]))
        copies[-1].start()

    eh, el = split(easts_ref[:loads, :])
    seh, sel = split(easts_ref[loads:, :])
    e = jnp.concatenate([eh, el], axis=0)
    se = jnp.concatenate([seh, sel], axis=0)
    sw = sibs_ref[SYSTEM + 2 * loads :, :]
    so = jnp.concatenate([sib_ref[B:, :B], sib_ref[B:, B : 2 * B]], axis=0)
    sknown = jnp.concatenate([jnp.where(low, se, so), jnp.where(low, so, se), sw], axis=1)
    ae = own_ref[:B, pl.ds(pl.multiple_of(B - parity * B, B), B)]
    applied = dot_t(e, ae) + dot_t(sknown, sib)
    solved = (dot(xh, sib) + dot(xl, sib)).astype(BF16)
    total = total + (applied[:loads] + applied[loads:])
    yh, yl = split(total)
    both = dot(jnp.concatenate([yh, yl], axis=0), xh)
    shared = -(both[:loads] + (both[loads:] + dot(yh, xl)))
    other(0)
    sh, sl = split(shared)
    hi = jnp.concatenate([eh, sh], axis=1)
    lo = jnp.concatenate([el, sl], axis=1)
    inner = dot_t(jnp.concatenate([hi, lo], axis=0), mh)
    other(1)
    values_ref[...] = base + inner[:loads] + (inner[loads:] + dot_t(hi, ml))
    other(2)
    for copy in copies:
        copy.wait()


def per_device(dtn, flux_part, point_order, west_values, outer_values, interior_map, interior_part):
    dtn, flux, order = dtn[0, 0], flux_part[0, 0], point_order[0]
    west, outer, imap, part = west_values[0, 0], outer_values[0, 0], interior_map[0, 0], interior_part[0, 0]
    full = dtn.shape[0]
    three = full - B
    loads = west.shape[0]
    count = three // lax.axis_size("cores")
    rows, cols = lax.axis_size("row"), lax.axis_size("col")
    pairs = [(i, i ^ 1) for i in range(rows)]
    shape = jax.ShapeDtypeStruct
    vm = pl.BlockSpec(memory_space=pltpu.VMEM)
    hbm = pl.BlockSpec(memory_space=pltpu.HBM)
    params = pltpu.CompilerParams(vmem_limit_bytes=LIMIT)
    dma = pltpu.SemaphoreType.DMA

    def cost(flops, moved):
        return pl.CostEstimate(flops=flops, bytes_accessed=moved, transcendentals=0)

    s_pack, a_pack, fluxed, pick, held = pl.pallas_call(
        gather_kernel,
        out_shape=(
            shape((SYSTEM + 4 * loads, B), BF16),
            shape((B + loads, three), BF16),
            shape((loads, full), F32),
            shape((full, full), BF16),
            shape((full, full), BF16),
        ),
        in_specs=[hbm] * 5,
        out_specs=(vm,) * 5,
        scratch_shapes=[
            pltpu.VMEM(order.shape, jnp.int32),
            pltpu.VMEM(flux.shape, F32),
            pltpu.VMEM(west.shape, F32),
            pltpu.VMEM(outer.shape, F32),
            dma((5,)),
        ],
        compiler_params=params,
        cost_estimate=cost(10**9, 4 * 10**6),
        name="gather_shared",
    )(*[in_hbm(array) for array in (order, dtn, flux, west, outer)])

    s_sib = lax.ppermute(s_pack, "row", pairs)
    a_sib = lax.ppermute(a_pack, "row", pairs)
    at = SYSTEM + 2 * loads
    def own_block(late):
        return pl.pallas_call(
            functools.partial(block_kernel, late),
            out_shape=(
                shape((count, three), BF16),
                shape((count, B), BF16),
                shape((B, 2 * B), BF16),
                shape((B, 2 * B), BF16),
                shape((B, full), BF16),
                shape((B, full), BF16),
            ),
            in_specs=[vm, vm, hbm],
            out_specs=(vm,) * 6,
            scratch_shapes=[pltpu.VMEM(imap.shape, F32), dma],
            compiler_params=params,
            cost_estimate=cost(2 * 10**9, 10**6),
            name="own_block",
        )(pick, held, in_hbm(imap))

    inverse_shapes = (
        shape((count, three), BF16),
        shape((B, B), BF16),
        shape((B, B), BF16),
        shape((loads, three), F32),
        shape((loads, B), F32),
        shape((loads, B), F32),
    )
    def inverse(kernel, *blocks):
        return pl.pallas_call(
            kernel,
            out_shape=inverse_shapes,
            in_specs=[vm] * (len(blocks) + 6),
            out_specs=(vm,) * 6,
            scratch_shapes=[pltpu.VMEM((B, B), F32)],
            compiler_params=params,
            cost_estimate=cost(4 * 10**9, 10**6),
            name="inverse",
        )(*blocks, s_pack, s_sib, a_pack, fluxed, pick, part)

    d, rows_j, mh, ml, ih, il = own_block(False)
    half, xh, xl, pflux, total, base = inverse(early_inverse_kernel, d, rows_j, ih, il)
    west_sib = s_sib[at : at + loads].astype(F32) + s_sib[at + loads : at + 2 * loads].astype(F32)
    wests = jnp.concatenate([west, west_sib], axis=0)
    wests, half, xh, pick, held = lax.optimization_barrier((wests, half, xh, pick, held))
    easts = lax.ppermute(wests, "col", [((i + 1) % cols, i) for i in range(cols)])

    d2, rows_j2, mh2, ml2, ih2, il2 = own_block(True)
    half2, xh2, xl2, pflux2, total2, base2 = inverse(
        late_inverse_kernel, d, rows_j, ih, il, d2, rows_j2, ih2, il2
    )

    parent, pflux, values = pl.pallas_call(
        merge_kernel,
        out_shape=(shape((count, 2 * three), BF16), shape((loads, three), F32), shape((loads, B), F32)),
        in_specs=[vm] * 22,
        out_specs=(hbm, vm, vm),
        scratch_shapes=[pltpu.VMEM((count, three), BF16), dma((4,))],
        compiler_params=params,
        cost_estimate=cost(10**9, 10**6),
        name="merge",
    )(
        a_pack, a_sib, s_sib, easts,
        half, xh, xl, pflux, total, base, rows_j, mh, ml,
        half2, xh2, xl2, pflux2, total2, base2, rows_j2, mh2, ml2,
    )
    return (parent[None, None], pflux[None, None], values[None, None])


def solution(mesh):
    box = P("row", "col", None, None)
    part = P("row", "col", "cores", None)
    return jax.shard_map(
        per_device,
        mesh=mesh,
        in_specs=(box, part, P("row", "col", None), part, part, box, part),
        out_specs=(part, part, part),
        check_vma=False,
    )
```

```python
import functools

import jax
import jax.numpy as jnp
from jax import lax
from jax.experimental import pallas as pl
from jax.experimental.pallas import tpu as pltpu
from jax.sharding import PartitionSpec as P

B = 256
F32 = jnp.float32
BF16 = jnp.bfloat16
LIMIT = 32 * 1024 * 1024
SYSTEM = 3 * B // 4


def dot(a, b):
    return lax.dot_general(a, b, (((1,), (0,)), ((), ())), preferred_element_type=F32)


def dot_t(a, b):
    return lax.dot_general(a, b, (((1,), (1,)), ((), ())), preferred_element_type=F32)


def split(x):
    high = x.astype(BF16)
    return high, (x - high.astype(F32)).astype(BF16)


def timed(a, b):
    rows = a.shape[0]
    both = dot(jnp.concatenate(split(a), axis=0), b)
    return both[:rows] + both[rows:]


def in_hbm(array):
    return pltpu.with_memory_space_constraint(array, pltpu.HBM)


def parity_of():
    return lax.rem(lax.axis_index("row"), 2)


def positions(order_ref, parity):
    low = parity == 0
    sides = [order_ref[:, s * B : (s + 1) * B] for s in range(4)]
    pos = jnp.concatenate(
        [
            jnp.where(low, sides[0], sides[1]),
            jnp.where(low, sides[1], sides[2]),
            sides[3],
            jnp.where(low, sides[2], sides[0]),
        ],
        axis=1,
    )
    return jnp.broadcast_to(pos, (8, pos.shape[1])).T[:, 0:1]


def one_hot(column, full):
    marks = lax.broadcasted_iota(jnp.int32, (column.shape[0], full), 1)
    return jnp.where(column == marks, 1.0, 0.0).astype(BF16)


def gather_kernel(
    order_hbm, dtn_hbm, flux_hbm, west_hbm,
    s_ref, rows_ref, pick_ref, map_ref,
    order_ref, flux_ref, west_ref, sems,
):
    copies = [
        pltpu.make_async_copy(source, target, sems.at[i])
        for i, (source, target) in enumerate(
            [
                (order_hbm, order_ref),
                (dtn_hbm, map_ref),
                (flux_hbm, flux_ref),
                (west_hbm, west_ref),
            ]
        )
    ]
    for copy in copies:
        copy.start()
    three = 3 * B
    loads = flux_ref.shape[0]
    copies[0].wait()
    pick = one_hot(positions(order_ref, parity_of()), map_ref.shape[0])
    pick_ref[...] = pick
    copies[1].wait()
    rows = dot(pick[three:], map_ref[...]).astype(BF16)
    copies[2].wait()
    rows_ref[:B, :] = rows
    fh, fl = split(flux_ref[...])
    rows_ref[B : B + loads, :] = fh
    rows_ref[B + loads :, :] = fl
    mine = dot_t(jnp.concatenate([rows, fh, fl], axis=0), pick[three:]).astype(BF16)
    half = B // 2
    s_ref[:half, :half] = mine[:half, :half]
    s_ref[:half, half:] = mine[half:B, half:]
    s_ref[half : B - half // 2, :half] = mine[half : B - half // 2, :half]
    s_ref[half : B - half // 2, half:] = mine[B - half // 2 : B, :half]
    s_ref[SYSTEM : SYSTEM + 2 * loads, :] = mine[B:]
    copies[3].wait()
    wh, wl = split(west_ref[...])
    s_ref[SYSTEM + 2 * loads : SYSTEM + 3 * loads, :] = wh
    s_ref[SYSTEM + 3 * loads :, :] = wl


def coupling_kernel(rows_ref, pick_ref, outer_ref, a_ref, fluxed_ref):
    three = 3 * B
    loads = outer_ref.shape[0]
    mine = dot_t(rows_ref[...], pick_ref[:three, :])
    for i in range(3):
        a_ref[i * B : (i + 1) * B, :] = mine[:B, i * B : (i + 1) * B].astype(BF16)
    oh, ol = split(outer_ref[...])
    a_ref[three : three + loads, :] = oh
    a_ref[three + loads :, :] = ol
    fluxed_ref[...] = mine[B : B + loads] + mine[B + loads :]


def own_body(pick_ref, map_ref, imap_hbm, d_ref, rowsj_ref, mh_ref, ml_ref, ih_ref, il_ref, imap_ref, sem):
    copy = pltpu.make_async_copy(imap_hbm, imap_ref, sem)
    copy.start()
    three = 3 * B
    count = d_ref.shape[0]
    start = pl.multiple_of(lax.axis_index("cores") * count, count)
    rows = dot(pick_ref[pl.ds(start, count), :], map_ref[...]).astype(BF16)
    block = dot_t(rows, pick_ref[...]).astype(BF16)
    d_ref[...] = block[:, :three]
    rowsj_ref[...] = block[:, three:]

    copy.wait()
    mh, ml = split(imap_ref[...])
    ih_ref[...] = mh
    il_ref[...] = ml
    pe = pick_ref[pl.ds(pl.multiple_of(B - parity_of() * B, B), B), :]
    picked = dot_t(jnp.concatenate([mh, ml], axis=0), jnp.concatenate([pe, pick_ref[three:, :]], axis=0))
    mh_ref[...] = picked[:B].astype(BF16)
    ml_ref[...] = picked[B:].astype(BF16)


def coupling_of(ref):
    return jnp.concatenate([ref[i * B : (i + 1) * B, :] for i in range(3)], axis=1)


def system_of(own_ref, sib_ref):
    half = B // 2
    parts = own_ref[:SYSTEM, :].astype(F32) + sib_ref[:SYSTEM, :].astype(F32)
    low = jnp.concatenate([parts[half:, :half], parts[half:, half:]], axis=0)
    return jnp.concatenate(
        [
            jnp.concatenate([parts[:half, :half], low.T], axis=1),
            jnp.concatenate([low, parts[:half, half:]], axis=1),
        ],
        axis=0,
    )


def inverse_body(
    d_ref, rowsj_ref, ih_ref, il_ref, own_ref, sib_ref, coup_ref, flux_ref, pick_ref, part_ref,
    half_ref, xh_ref, xl_ref, pflux_ref, total_ref, base_ref,
    x_ref,
):
    three = 3 * B
    loads = flux_ref.shape[0]
    parity = parity_of()
    coup = coupling_of(coup_ref)
    west = own_ref[SYSTEM + 2 * loads :, :]
    outer = coup_ref[three:, :]
    eye = jnp.where(
        lax.broadcasted_iota(jnp.int32, (B, B), 0) == lax.broadcasted_iota(jnp.int32, (B, B), 1), 1.0, 0.0
    ).astype(F32)

    system = system_of(own_ref, sib_ref)
    top = jnp.max(jnp.sum(jnp.abs(system), axis=0, keepdims=True), axis=1, keepdims=True)
    alpha = 1.0 / top
    low = 1.0 / 128
    scales = []
    for _ in range(5):
        scales.append(2.0 / (1.0 + low))
        low = 4.0 * low / (1.0 + low) ** 2

    def first(state):
        t = system * (alpha * scales[0])
        n = (eye - t).astype(BF16)
        return t + timed(t, n), (alpha * scales[0]) * (eye + n.astype(F32))

    def step(c):
        def one(state):
            both = c * jnp.concatenate(state, axis=0)
            n = (eye - both[:B]).astype(BF16)
            both = both + timed(both, n)
            return both[:B], both[B:]

        return one

    po = pick_ref[pl.ds(pl.multiple_of(parity * B, B), B), :]
    pw = pick_ref[2 * B : three, :]
    mh = ih_ref[...]
    state = first(None)
    stored = dot(outer, po)
    state = step(scales[1])(state)
    stored = (stored + dot(west, pw)).astype(BF16)
    state = step(scales[2])(state)
    inner = dot_t(stored, mh)
    state = step(scales[3])(state)
    base_ref[...] = part_ref[...] + inner[:loads] + (inner[loads:] + dot_t(stored[:loads], il_ref[...]))
    t, x = step(scales[4])(state)
    x = x + timed(x, (eye - t).astype(BF16))
    sh, sl = split(system)
    xh, xl = split(x)
    high = dot(jnp.concatenate([sh, sl], axis=0), xh)
    res = eye - (high[:B] + (high[B:] + dot(sh, xl)))

    ao = coup_ref[pl.ds(pl.multiple_of(parity * B, B), B), :]
    aw = coup[:, 2 * B :]
    applied = dot_t(outer, ao) + dot_t(west, aw)
    x_ref[...] = x + dot(xh, res.astype(BF16))
    off = jnp.max(jnp.sum(jnp.abs(res), axis=0))
    at = slice(SYSTEM, SYSTEM + 2 * loads)
    fluxes = own_ref[at, :].astype(F32) + sib_ref[at, :].astype(F32)
    edge = fluxes[:loads] + fluxes[loads:]
    total_ref[...] = edge + (applied[:loads] + applied[loads:])

    @pl.when(jnp.logical_not(off < 0.005))
    def _():
        def exact(a, b):
            return lax.dot_general(
                a, b, (((1,), (0,)), ((), ())), precision=lax.Precision.HIGHEST, preferred_element_type=F32
            )

        def body(state):
            step, _ = state
            x = x_ref[...]
            r = eye - exact(system, x)
            x_ref[...] = x + exact(x, r)
            return step + 1, jnp.max(jnp.sum(jnp.abs(r), axis=0))

        x_ref[...] = eye * alpha
        lax.while_loop(
            lambda state: jnp.logical_and(state[0] < 64, jnp.logical_not(state[1] < 0.001)),
            body,
            (jnp.int32(0), jnp.float32(1.0)),
        )

    xh, xl = split(x_ref[...])
    xh_ref[...] = xh
    xl_ref[...] = xl
    eh, el = split(edge)
    both = dot(jnp.concatenate([eh, el], axis=0), xh)
    zeta = both[:loads] + (both[loads:] + dot(eh, xl))
    solved = (dot(xh, coup) + dot(xl, coup)).astype(BF16)
    zh, zl = split(zeta)
    moved = dot(jnp.concatenate([zh, zl], axis=0), coup)
    half_ref[...] = (d_ref[...].astype(F32) - dot(rowsj_ref[...], solved)).astype(BF16)
    pflux_ref[...] = flux_ref[...] - (moved[:loads] + moved[loads:])


def late_block():
    row, col, core = lax.axis_index("row"), lax.axis_index("col"), lax.axis_index("cores")
    return jnp.logical_or(col > lax.axis_size("col") // 2, row + col + core == 0)


def late_inverse():
    return jnp.logical_or(late_block(), lax.axis_index("col") == lax.axis_size("col") // 2)


def block_kernel(late, *refs):
    there = late_block()

    @pl.when(there if late else jnp.logical_not(there))
    def _():
        own_body(*refs)


def early_inverse_kernel(*refs):
    @pl.when(jnp.logical_not(late_inverse()))
    def _():
        inverse_body(*refs)


def late_inverse_kernel(*refs):
    there = late_block()

    @pl.when(there)
    def _():
        inverse_body(*refs[4:])

    @pl.when(jnp.logical_and(late_inverse(), jnp.logical_not(there)))
    def _():
        inverse_body(*refs[:4], *refs[8:])


def merge_kernel(own_ref, sib_ref, sibs_ref, easts_ref, *refs):
    first, second, (parent_hbm, pflux_ref, values_ref, other_ref, sems) = refs[:9], refs[9:18], refs[18:]
    three = 3 * B
    loads = values_ref.shape[0]
    parity = parity_of()
    low = parity == 0
    here, there = late_inverse(), late_block()
    target = parent_hbm.at[:, pl.ds(pl.multiple_of(parity * three, three), three)]
    copies = [pltpu.make_async_copy(first[0], target, sems.at[3])]

    @pl.when(jnp.logical_not(here))
    def _():
        copies[0].start()

    @pl.when(here)
    def _():
        pltpu.make_async_copy(second[0], target, sems.at[3]).start()

    xh, xl, pflux, total, base = [jnp.where(here, b[...], a[...]) for a, b in zip(first[1:6], second[1:6])]
    rows_j, mh, ml = [jnp.where(there, b[...], a[...]) for a, b in zip(first[6:], second[6:])]
    pflux_ref[...] = pflux
    sib = coupling_of(sib_ref)
    at = pl.multiple_of(three - parity * three, B)
    size = other_ref.shape[0] // 3

    def other(i):
        part = slice(i * size, (i + 1) * size)
        other_ref[part] = (-dot(rows_j[part], solved)).astype(BF16)
        copies.append(pltpu.make_async_copy(other_ref.at[part], parent_hbm.at[part, pl.ds(at, three)], sems.at[i]))
        copies[-1].start()

    eh, el = split(easts_ref[:loads, :])
    seh, sel = split(easts_ref[loads:, :])
    e = jnp.concatenate([eh, el], axis=0)
    se = jnp.concatenate([seh, sel], axis=0)
    sw = sibs_ref[SYSTEM + 2 * loads :, :]
    so = sib_ref[three:, :]
    sknown = jnp.concatenate([jnp.where(low, se, so), jnp.where(low, so, se), sw], axis=1)
    ae = own_ref[pl.ds(pl.multiple_of(B - parity * B, B), B), :]
    applied = dot_t(e, ae) + dot_t(sknown, sib)
    solved = (dot(xh, sib) + dot(xl, sib)).astype(BF16)
    total = total + (applied[:loads] + applied[loads:])
    yh, yl = split(total)
    both = dot(jnp.concatenate([yh, yl], axis=0), xh)
    shared = -(both[:loads] + (both[loads:] + dot(yh, xl)))
    other(0)
    sh, sl = split(shared)
    hi = jnp.concatenate([eh, sh], axis=1)
    lo = jnp.concatenate([el, sl], axis=1)
    inner = dot_t(jnp.concatenate([hi, lo], axis=0), mh)
    other(1)
    values_ref[...] = base + inner[:loads] + (inner[loads:] + dot_t(hi, ml))
    other(2)
    for copy in copies:
        copy.wait()


def per_device(dtn, flux_part, point_order, west_values, outer_values, interior_map, interior_part):
    dtn, flux, order = dtn[0, 0], flux_part[0, 0], point_order[0]
    west, outer, imap, part = west_values[0, 0], outer_values[0, 0], interior_map[0, 0], interior_part[0, 0]
    full = dtn.shape[0]
    three = full - B
    loads = west.shape[0]
    count = three // lax.axis_size("cores")
    rows, cols = lax.axis_size("row"), lax.axis_size("col")
    pairs = [(i, i ^ 1) for i in range(rows)]
    shape = jax.ShapeDtypeStruct
    vm = pl.BlockSpec(memory_space=pltpu.VMEM)
    hbm = pl.BlockSpec(memory_space=pltpu.HBM)
    params = pltpu.CompilerParams(vmem_limit_bytes=LIMIT)
    dma = pltpu.SemaphoreType.DMA

    def cost(flops, moved):
        return pl.CostEstimate(flops=flops, bytes_accessed=moved, transcendentals=0)

    s_pack, gathered, pick, held = pl.pallas_call(
        gather_kernel,
        out_shape=(
            shape((SYSTEM + 4 * loads, B), BF16),
            shape((B + 2 * loads, full), BF16),
            shape((full, full), BF16),
            shape((full, full), BF16),
        ),
        in_specs=[hbm] * 4,
        out_specs=(vm,) * 4,
        scratch_shapes=[
            pltpu.VMEM(order.shape, jnp.int32),
            pltpu.VMEM(flux.shape, F32),
            pltpu.VMEM(west.shape, F32),
            dma((4,)),
        ],
        compiler_params=params,
        cost_estimate=cost(10**9, 4 * 10**6),
        name="gather_shared",
    )(*[in_hbm(array) for array in (order, dtn, flux, west)])

    a_pack, fluxed = pl.pallas_call(
        coupling_kernel,
        out_shape=(shape((three + 2 * loads, B), BF16), shape((loads, three), F32)),
        in_specs=[vm] * 3,
        out_specs=(vm,) * 2,
        compiler_params=params,
        cost_estimate=cost(5 * 10**8, 10**6),
        name="coupling",
    )(gathered, pick, outer)

    s_sib = lax.ppermute(s_pack, "row", pairs)
    a_sib = lax.ppermute(a_pack, "row", pairs)
    at = SYSTEM + 2 * loads
    def own_block(late):
        return pl.pallas_call(
            functools.partial(block_kernel, late),
            out_shape=(
                shape((count, three), BF16),
                shape((count, B), BF16),
                shape((B, 2 * B), BF16),
                shape((B, 2 * B), BF16),
                shape((B, full), BF16),
                shape((B, full), BF16),
            ),
            in_specs=[vm, vm, hbm],
            out_specs=(vm,) * 6,
            scratch_shapes=[pltpu.VMEM(imap.shape, F32), dma],
            compiler_params=params,
            cost_estimate=cost(2 * 10**9, 10**6),
            name="own_block",
        )(pick, held, in_hbm(imap))

    inverse_shapes = (
        shape((count, three), BF16),
        shape((B, B), BF16),
        shape((B, B), BF16),
        shape((loads, three), F32),
        shape((loads, B), F32),
        shape((loads, B), F32),
    )
    def inverse(kernel, *blocks):
        return pl.pallas_call(
            kernel,
            out_shape=inverse_shapes,
            in_specs=[vm] * (len(blocks) + 6),
            out_specs=(vm,) * 6,
            scratch_shapes=[pltpu.VMEM((B, B), F32)],
            compiler_params=params,
            cost_estimate=cost(4 * 10**9, 10**6),
            name="inverse",
        )(*blocks, s_pack, s_sib, a_pack, fluxed, pick, part)

    d, rows_j, mh, ml, ih, il = own_block(False)
    half, xh, xl, pflux, total, base = inverse(early_inverse_kernel, d, rows_j, ih, il)
    west_sib = s_sib[at : at + loads].astype(F32) + s_sib[at + loads : at + 2 * loads].astype(F32)
    wests = jnp.concatenate([west, west_sib], axis=0)
    wests, half, xh, pick, held = lax.optimization_barrier((wests, half, xh, pick, held))
    easts = lax.ppermute(wests, "col", [((i + 1) % cols, i) for i in range(cols)])

    d2, rows_j2, mh2, ml2, ih2, il2 = own_block(True)
    half2, xh2, xl2, pflux2, total2, base2 = inverse(
        late_inverse_kernel, d, rows_j, ih, il, d2, rows_j2, ih2, il2
    )

    parent, pflux, values = pl.pallas_call(
        merge_kernel,
        out_shape=(shape((count, 2 * three), BF16), shape((loads, three), F32), shape((loads, B), F32)),
        in_specs=[vm] * 22,
        out_specs=(hbm, vm, vm),
        scratch_shapes=[pltpu.VMEM((count, three), BF16), dma((4,))],
        compiler_params=params,
        cost_estimate=cost(10**9, 10**6),
        name="merge",
    )(
        a_pack, a_sib, s_sib, easts,
        half, xh, xl, pflux, total, base, rows_j, mh, ml,
        half2, xh2, xl2, pflux2, total2, base2, rows_j2, mh2, ml2,
    )
    return (parent[None, None], pflux[None, None], values[None, None])


def solution(mesh):
    box = P("row", "col", None, None)
    part = P("row", "col", "cores", None)
    return jax.shard_map(
        per_device,
        mesh=mesh,
        in_specs=(box, part, P("row", "col", None), part, part, box, part),
        out_specs=(part, part, part),
        check_vma=False,
    )
```

```python
import functools

import jax
import jax.numpy as jnp
from jax import lax
from jax.experimental import pallas as pl
from jax.experimental.pallas import tpu as pltpu
from jax.sharding import PartitionSpec as P

B = 256
F32 = jnp.float32
BF16 = jnp.bfloat16
LIMIT = 32 * 1024 * 1024
SYSTEM = 5 * B // 8


def dot(a, b):
    return lax.dot_general(a, b, (((1,), (0,)), ((), ())), preferred_element_type=F32)


def dot_t(a, b):
    return lax.dot_general(a, b, (((1,), (1,)), ((), ())), preferred_element_type=F32)


def split(x):
    high = x.astype(BF16)
    return high, (x - high.astype(F32)).astype(BF16)


def timed(a, b):
    rows = a.shape[0]
    both = dot(jnp.concatenate(split(a), axis=0), b)
    return both[:rows] + both[rows:]


def in_hbm(array):
    return pltpu.with_memory_space_constraint(array, pltpu.HBM)


def parity_of():
    return lax.rem(lax.axis_index("row"), 2)


def positions(order_ref, parity):
    low = parity == 0
    sides = [order_ref[:, s * B : (s + 1) * B] for s in range(4)]
    pos = jnp.concatenate(
        [
            jnp.where(low, sides[0], sides[1]),
            jnp.where(low, sides[1], sides[2]),
            sides[3],
            jnp.where(low, sides[2], sides[0]),
        ],
        axis=1,
    )
    return jnp.broadcast_to(pos, (8, pos.shape[1])).T[:, 0:1]


def one_hot(column, full):
    marks = lax.broadcasted_iota(jnp.int32, (column.shape[0], full), 1)
    return jnp.where(column == marks, 1.0, 0.0).astype(BF16)


def gather_kernel(
    order_hbm, dtn_hbm, flux_hbm, west_hbm,
    s_ref, rows_ref, pick_ref, map_ref,
    order_ref, flux_ref, west_ref, sems,
):
    copies = [
        pltpu.make_async_copy(source, target, sems.at[i])
        for i, (source, target) in enumerate(
            [
                (order_hbm, order_ref),
                (dtn_hbm, map_ref),
                (flux_hbm, flux_ref),
                (west_hbm, west_ref),
            ]
        )
    ]
    for copy in copies:
        copy.start()
    three = 3 * B
    loads = flux_ref.shape[0]
    copies[0].wait()
    pick = one_hot(positions(order_ref, parity_of()), map_ref.shape[0])
    pick_ref[...] = pick
    copies[1].wait()
    rows = dot(pick[three:], map_ref[...]).astype(BF16)
    copies[2].wait()
    rows_ref[:B, :] = rows
    fh, fl = split(flux_ref[...])
    rows_ref[B : B + loads, :] = fh
    rows_ref[B + loads :, :] = fl
    mine = dot_t(jnp.concatenate([rows, fh, fl], axis=0), pick[three:]).astype(BF16)
    n = B // 4

    def piece(i, j):
        return mine[i * n : (i + 1) * n, j * n : (j + 1) * n]

    a, b = piece(2, 0), piece(3, 1)
    h = n // 2
    s_ref[:n, :] = jnp.concatenate([piece(i, i) for i in range(4)], axis=1)
    s_ref[n : 2 * n, :] = jnp.concatenate([piece(1, 0), piece(2, 1), piece(3, 2), piece(3, 0)], axis=1)
    s_ref[2 * n : SYSTEM, :] = jnp.concatenate([a[:h], b[:h], a[h:], b[h:]], axis=1)
    s_ref[SYSTEM : SYSTEM + 2 * loads, :] = mine[B:]
    copies[3].wait()
    wh, wl = split(west_ref[...])
    s_ref[SYSTEM + 2 * loads : SYSTEM + 3 * loads, :] = wh
    s_ref[SYSTEM + 3 * loads :, :] = wl


def coupling_kernel(rows_ref, pick_ref, outer_ref, a_ref, fluxed_ref):
    three = 3 * B
    loads = outer_ref.shape[0]
    mine = dot_t(rows_ref[...], pick_ref[:three, :])
    for i in range(3):
        a_ref[i * B : (i + 1) * B, :] = mine[:B, i * B : (i + 1) * B].astype(BF16)
    oh, ol = split(outer_ref[...])
    a_ref[three : three + loads, :] = oh
    a_ref[three + loads :, :] = ol
    fluxed_ref[...] = mine[B : B + loads] + mine[B + loads :]


def own_body(pick_ref, map_ref, imap_hbm, d_ref, rowsj_ref, mh_ref, ml_ref, ih_ref, il_ref, imap_ref, sem):
    copy = pltpu.make_async_copy(imap_hbm, imap_ref, sem)
    copy.start()
    three = 3 * B
    count = d_ref.shape[0]
    start = pl.multiple_of(lax.axis_index("cores") * count, count)
    rows = dot(pick_ref[pl.ds(start, count), :], map_ref[...]).astype(BF16)
    block = dot_t(rows, pick_ref[...]).astype(BF16)
    d_ref[...] = block[:, :three]
    rowsj_ref[...] = block[:, three:]

    copy.wait()
    mh, ml = split(imap_ref[...])
    ih_ref[...] = mh
    il_ref[...] = ml
    pe = pick_ref[pl.ds(pl.multiple_of(B - parity_of() * B, B), B), :]
    picked = dot_t(jnp.concatenate([mh, ml], axis=0), jnp.concatenate([pe, pick_ref[three:, :]], axis=0))
    mh_ref[...] = picked[:B].astype(BF16)
    ml_ref[...] = picked[B:].astype(BF16)


def coupling_of(ref):
    return jnp.concatenate([ref[i * B : (i + 1) * B, :] for i in range(3)], axis=1)


def system_of(own_ref, sib_ref):
    n, h = B // 4, B // 8
    parts = own_ref[:SYSTEM, :].astype(F32) + sib_ref[:SYSTEM, :].astype(F32)

    def piece(k, j, rows=n):
        return parts[k * n : k * n + rows, j * n : (j + 1) * n]

    zero = jnp.zeros((n, n), F32)
    a = jnp.concatenate([piece(2, 0, h), piece(2, 2, h)], axis=0)
    b = jnp.concatenate([piece(2, 1, h), piece(2, 3, h)], axis=0)
    diagonal = [[piece(0, i) if i == j else zero for j in range(4)] for i in range(4)]
    lower = [
        [zero] * 4,
        [piece(1, 0), zero, zero, zero],
        [a, piece(1, 1), zero, zero],
        [piece(1, 3), b, piece(1, 2), zero],
    ]
    diagonal, lower = [
        jnp.concatenate([jnp.concatenate(row, axis=1) for row in blocks], axis=0) for blocks in (diagonal, lower)
    ]
    return diagonal + (lower + lower.T)


def inverse_body(
    d_ref, rowsj_ref, ih_ref, il_ref, own_ref, sib_ref, coup_ref, flux_ref, pick_ref, part_ref,
    half_ref, xh_ref, xl_ref, pflux_ref, total_ref, base_ref,
    x_ref,
):
    three = 3 * B
    loads = flux_ref.shape[0]
    parity = parity_of()
    coup = coupling_of(coup_ref)
    west = own_ref[SYSTEM + 2 * loads :, :]
    outer = coup_ref[three:, :]
    eye = jnp.where(
        lax.broadcasted_iota(jnp.int32, (B, B), 0) == lax.broadcasted_iota(jnp.int32, (B, B), 1), 1.0, 0.0
    ).astype(F32)

    system = system_of(own_ref, sib_ref)
    top = jnp.max(jnp.sum(jnp.abs(system), axis=0, keepdims=True), axis=1, keepdims=True)
    alpha = 1.0 / top
    low = 1.0 / 128
    scales = []
    for _ in range(5):
        scales.append(2.0 / (1.0 + low))
        low = 4.0 * low / (1.0 + low) ** 2

    def first(state):
        t = system * (alpha * scales[0])
        n = (eye - t).astype(BF16)
        return t + timed(t, n), (alpha * scales[0]) * (eye + n.astype(F32))

    def step(c):
        def one(state):
            both = c * jnp.concatenate(state, axis=0)
            n = (eye - both[:B]).astype(BF16)
            both = both + timed(both, n)
            return both[:B], both[B:]

        return one

    po = pick_ref[pl.ds(pl.multiple_of(parity * B, B), B), :]
    pw = pick_ref[2 * B : three, :]
    mh = ih_ref[...]
    state = first(None)
    stored = dot(outer, po)
    state = step(scales[1])(state)
    stored = (stored + dot(west, pw)).astype(BF16)
    state = step(scales[2])(state)
    inner = dot_t(stored, mh)
    state = step(scales[3])(state)
    base_ref[...] = part_ref[...] + inner[:loads] + (inner[loads:] + dot_t(stored[:loads], il_ref[...]))
    t, x = step(scales[4])(state)
    x = x + timed(x, (eye - t).astype(BF16))
    sh, sl = split(system)
    xh, xl = split(x)
    high = dot(jnp.concatenate([sh, sl], axis=0), xh)
    res = eye - (high[:B] + (high[B:] + dot(sh, xl)))

    ao = coup_ref[pl.ds(pl.multiple_of(parity * B, B), B), :]
    aw = coup[:, 2 * B :]
    applied = dot_t(outer, ao) + dot_t(west, aw)
    x_ref[...] = x + dot(xh, res.astype(BF16))
    off = jnp.max(jnp.sum(jnp.abs(res), axis=0))
    at = slice(SYSTEM, SYSTEM + 2 * loads)
    fluxes = own_ref[at, :].astype(F32) + sib_ref[at, :].astype(F32)
    edge = fluxes[:loads] + fluxes[loads:]
    total_ref[...] = edge + (applied[:loads] + applied[loads:])

    @pl.when(jnp.logical_not(off < 0.005))
    def _():
        def exact(a, b):
            return lax.dot_general(
                a, b, (((1,), (0,)), ((), ())), precision=lax.Precision.HIGHEST, preferred_element_type=F32
            )

        def body(state):
            step, _ = state
            x = x_ref[...]
            r = eye - exact(system, x)
            x_ref[...] = x + exact(x, r)
            return step + 1, jnp.max(jnp.sum(jnp.abs(r), axis=0))

        x_ref[...] = eye * alpha
        lax.while_loop(
            lambda state: jnp.logical_and(state[0] < 64, jnp.logical_not(state[1] < 0.001)),
            body,
            (jnp.int32(0), jnp.float32(1.0)),
        )

    xh, xl = split(x_ref[...])
    xh_ref[...] = xh
    xl_ref[...] = xl
    eh, el = split(edge)
    both = dot(jnp.concatenate([eh, el], axis=0), xh)
    zeta = both[:loads] + (both[loads:] + dot(eh, xl))
    solved = (dot(xh, coup) + dot(xl, coup)).astype(BF16)
    zh, zl = split(zeta)
    moved = dot(jnp.concatenate([zh, zl], axis=0), coup)
    half_ref[...] = (d_ref[...].astype(F32) - dot(rowsj_ref[...], solved)).astype(BF16)
    pflux_ref[...] = flux_ref[...] - (moved[:loads] + moved[loads:])


def late_block():
    row, col, core = lax.axis_index("row"), lax.axis_index("col"), lax.axis_index("cores")
    return jnp.logical_or(col > lax.axis_size("col") // 2, row + col + core == 0)


def late_inverse():
    return jnp.logical_or(late_block(), lax.axis_index("col") == lax.axis_size("col") // 2)


def block_kernel(late, *refs):
    there = late_block()

    @pl.when(there if late else jnp.logical_not(there))
    def _():
        own_body(*refs)


def early_inverse_kernel(*refs):
    @pl.when(jnp.logical_not(late_inverse()))
    def _():
        inverse_body(*refs)


def late_inverse_kernel(*refs):
    there = late_block()

    @pl.when(there)
    def _():
        inverse_body(*refs[4:])

    @pl.when(jnp.logical_and(late_inverse(), jnp.logical_not(there)))
    def _():
        inverse_body(*refs[:4], *refs[8:])


def merge_kernel(own_ref, sib_ref, sibs_ref, easts_ref, *refs):
    first, second, (parent_hbm, pflux_ref, values_ref, other_ref, sems) = refs[:9], refs[9:18], refs[18:]
    three = 3 * B
    loads = values_ref.shape[0]
    parity = parity_of()
    low = parity == 0
    here, there = late_inverse(), late_block()
    target = parent_hbm.at[:, pl.ds(pl.multiple_of(parity * three, three), three)]
    copies = [pltpu.make_async_copy(first[0], target, sems.at[3])]

    @pl.when(jnp.logical_not(here))
    def _():
        copies[0].start()

    @pl.when(here)
    def _():
        pltpu.make_async_copy(second[0], target, sems.at[3]).start()

    xh, xl, pflux, total, base = [jnp.where(here, b[...], a[...]) for a, b in zip(first[1:6], second[1:6])]
    rows_j, mh, ml = [jnp.where(there, b[...], a[...]) for a, b in zip(first[6:], second[6:])]
    pflux_ref[...] = pflux
    sib = coupling_of(sib_ref)
    at = pl.multiple_of(three - parity * three, B)
    size = other_ref.shape[0] // 3

    def other(i):
        part = slice(i * size, (i + 1) * size)
        other_ref[part] = (-dot(rows_j[part], solved)).astype(BF16)
        copies.append(pltpu.make_async_copy(other_ref.at[part], parent_hbm.at[part, pl.ds(at, three)], sems.at[i]))
        copies[-1].start()

    eh, el = split(easts_ref[:loads, :])
    seh, sel = split(easts_ref[loads:, :])
    e = jnp.concatenate([eh, el], axis=0)
    se = jnp.concatenate([seh, sel], axis=0)
    sw = sibs_ref[SYSTEM + 2 * loads :, :]
    so = sib_ref[three:, :]
    sknown = jnp.concatenate([jnp.where(low, se, so), jnp.where(low, so, se), sw], axis=1)
    ae = own_ref[pl.ds(pl.multiple_of(B - parity * B, B), B), :]
    applied = dot_t(e, ae) + dot_t(sknown, sib)
    solved = (dot(xh, sib) + dot(xl, sib)).astype(BF16)
    total = total + (applied[:loads] + applied[loads:])
    yh, yl = split(total)
    both = dot(jnp.concatenate([yh, yl], axis=0), xh)
    shared = -(both[:loads] + (both[loads:] + dot(yh, xl)))
    other(0)
    sh, sl = split(shared)
    hi = jnp.concatenate([eh, sh], axis=1)
    lo = jnp.concatenate([el, sl], axis=1)
    inner = dot_t(jnp.concatenate([hi, lo], axis=0), mh)
    other(1)
    values_ref[...] = base + inner[:loads] + (inner[loads:] + dot_t(hi, ml))
    other(2)
    for copy in copies:
        copy.wait()


def per_device(dtn, flux_part, point_order, west_values, outer_values, interior_map, interior_part):
    dtn, flux, order = dtn[0, 0], flux_part[0, 0], point_order[0]
    west, outer, imap, part = west_values[0, 0], outer_values[0, 0], interior_map[0, 0], interior_part[0, 0]
    full = dtn.shape[0]
    three = full - B
    loads = west.shape[0]
    count = three // lax.axis_size("cores")
    rows, cols = lax.axis_size("row"), lax.axis_size("col")
    pairs = [(i, i ^ 1) for i in range(rows)]
    shape = jax.ShapeDtypeStruct
    vm = pl.BlockSpec(memory_space=pltpu.VMEM)
    hbm = pl.BlockSpec(memory_space=pltpu.HBM)
    params = pltpu.CompilerParams(vmem_limit_bytes=LIMIT)
    dma = pltpu.SemaphoreType.DMA

    def cost(flops, moved):
        return pl.CostEstimate(flops=flops, bytes_accessed=moved, transcendentals=0)

    s_pack, gathered, pick, held = pl.pallas_call(
        gather_kernel,
        out_shape=(
            shape((SYSTEM + 4 * loads, B), BF16),
            shape((B + 2 * loads, full), BF16),
            shape((full, full), BF16),
            shape((full, full), BF16),
        ),
        in_specs=[hbm] * 4,
        out_specs=(vm,) * 4,
        scratch_shapes=[
            pltpu.VMEM(order.shape, jnp.int32),
            pltpu.VMEM(flux.shape, F32),
            pltpu.VMEM(west.shape, F32),
            dma((4,)),
        ],
        compiler_params=params,
        cost_estimate=cost(10**9, 4 * 10**6),
        name="gather_shared",
    )(*[in_hbm(array) for array in (order, dtn, flux, west)])

    a_pack, fluxed = pl.pallas_call(
        coupling_kernel,
        out_shape=(shape((three + 2 * loads, B), BF16), shape((loads, three), F32)),
        in_specs=[vm] * 3,
        out_specs=(vm,) * 2,
        compiler_params=params,
        cost_estimate=cost(5 * 10**8, 10**6),
        name="coupling",
    )(gathered, pick, outer)

    s_sib = lax.ppermute(s_pack, "row", pairs)
    a_sib = lax.ppermute(a_pack, "row", pairs)
    at = SYSTEM + 2 * loads
    def own_block(late):
        return pl.pallas_call(
            functools.partial(block_kernel, late),
            out_shape=(
                shape((count, three), BF16),
                shape((count, B), BF16),
                shape((B, 2 * B), BF16),
                shape((B, 2 * B), BF16),
                shape((B, full), BF16),
                shape((B, full), BF16),
            ),
            in_specs=[vm, vm, hbm],
            out_specs=(vm,) * 6,
            scratch_shapes=[pltpu.VMEM(imap.shape, F32), dma],
            compiler_params=params,
            cost_estimate=cost(2 * 10**9, 10**6),
            name="own_block",
        )(pick, held, in_hbm(imap))

    inverse_shapes = (
        shape((count, three), BF16),
        shape((B, B), BF16),
        shape((B, B), BF16),
        shape((loads, three), F32),
        shape((loads, B), F32),
        shape((loads, B), F32),
    )
    def inverse(kernel, *blocks):
        return pl.pallas_call(
            kernel,
            out_shape=inverse_shapes,
            in_specs=[vm] * (len(blocks) + 6),
            out_specs=(vm,) * 6,
            scratch_shapes=[pltpu.VMEM((B, B), F32)],
            compiler_params=params,
            cost_estimate=cost(4 * 10**9, 10**6),
            name="inverse",
        )(*blocks, s_pack, s_sib, a_pack, fluxed, pick, part)

    d, rows_j, mh, ml, ih, il = own_block(False)
    half, xh, xl, pflux, total, base = inverse(early_inverse_kernel, d, rows_j, ih, il)
    west_sib = s_sib[at : at + loads].astype(F32) + s_sib[at + loads : at + 2 * loads].astype(F32)
    wests = jnp.concatenate([west, west_sib], axis=0)
    wests, half, xh, pick, held = lax.optimization_barrier((wests, half, xh, pick, held))
    easts = lax.ppermute(wests, "col", [((i + 1) % cols, i) for i in range(cols)])

    d2, rows_j2, mh2, ml2, ih2, il2 = own_block(True)
    half2, xh2, xl2, pflux2, total2, base2 = inverse(
        late_inverse_kernel, d, rows_j, ih, il, d2, rows_j2, ih2, il2
    )

    parent, pflux, values = pl.pallas_call(
        merge_kernel,
        out_shape=(shape((count, 2 * three), BF16), shape((loads, three), F32), shape((loads, B), F32)),
        in_specs=[vm] * 22,
        out_specs=(hbm, vm, vm),
        scratch_shapes=[pltpu.VMEM((count, three), BF16), dma((4,))],
        compiler_params=params,
        cost_estimate=cost(10**9, 10**6),
        name="merge",
    )(
        a_pack, a_sib, s_sib, easts,
        half, xh, xl, pflux, total, base, rows_j, mh, ml,
        half2, xh2, xl2, pflux2, total2, base2, rows_j2, mh2, ml2,
    )
    return (parent[None, None], pflux[None, None], values[None, None])


def solution(mesh):
    box = P("row", "col", None, None)
    part = P("row", "col", "cores", None)
    return jax.shard_map(
        per_device,
        mesh=mesh,
        in_specs=(box, part, P("row", "col", None), part, part, box, part),
        out_specs=(part, part, part),
        check_vma=False,
    )
```
